32 devices in a mesh: group: 4 (over y, core), leaf: 8 (over z, x).
Axes of the slice: x: 2, y: 2, z: 4, core: 2. Of those that a mesh axis runs over, the one named last changes fastest.
Arguments:
- left_vectors: float32 [256, 128], replicated, may hold values from -6 to 6
- panel_vectors: bfloat16 [2, 256, 128], replicated, may hold values from -0.375 to 0.375
- panel_factors: float32 [2, 128, 128], replicated, may hold values from -0.5 to 0.5
- node_y: bfloat16 [4, 8, 5, 256, 256], P('group', 'leaf')
- node_t: float32 [4, 8, 5, 128, 256], P('group', 'leaf'), as said below
- leaf_v: bfloat16 [16384, 256], P(('group', 'leaf')), may hold values from -0.375 to 0.375
- leaf_t: float32 [4, 8, 256, 256], P('group', 'leaf'), may hold values from -0.1875 to 0.1875
- leaf_map: int32 [4, 8], P('group', 'leaf'), may hold values from 0 to 7, as said below
Outputs:
- eofs: bfloat16 [16384, 128], P(('group', 'leaf'))
The draws below stay inside these ranges and needn't reach their ends.
Inputs may be any that keep to these rules, and one draw needn't show every extreme that they name: leaf_map[g, s] is the leaf index of the device of group g that holds leaf slot s; slots 2m and 2m + 1 name devices 2m and 2m + 1 in either order. Every device that a node of level l covers holds the same node_y[., ., l]; every device in the first half of the node's devices holds the same node_t[., ., l], and so does every device in the second half.
All inputs are finite; a program needn't handle non-finite values.
Results may differ from the reference program's by a relative error of at most 0.0045.
Values sent between devices are 32-bit elements; how exact they have to be, the bound alone decides.
A program may use at most 64 MiB of HBM per device.

```python
import jax
import jax.numpy as jnp
from jax import lax

NSNAP = 256
KVEC = 128
PANEL = 128
ROWS_DEV = 512
PANELS = 2
GROUPS = 4
SLOTS = 8
LEVELS = 5
ROWS = 16384


def node_codes():
    device_total = GROUPS * SLOTS
    device = jnp.arange(device_total, dtype=jnp.int32)[:, None]
    tree_level = jnp.arange(LEVELS, dtype=jnp.int32)[None, :]
    block_size = jnp.right_shift(jnp.int32(device_total), tree_level)
    node_number = device // block_size
    lower_side = (device % block_size >= block_size // 2).astype(jnp.int32)
    codes = tree_level * device_total + node_number
    return (codes.reshape(-1), lower_side.reshape(-1))


def draw_node_t(key, part):
    codes, lower_side = node_codes()

    def draw_one(code, side_bit):
        sub_key = jax.random.fold_in(jax.random.fold_in(key, 11), code * 2 + side_bit)
        return jax.random.normal(sub_key, (NSNAP // 2, NSNAP), jnp.float32) * (4.0 * NSNAP) ** (-0.5)
    drawn = jax.vmap(draw_one)(codes, lower_side)
    return drawn.reshape(GROUPS, SLOTS, LEVELS, NSNAP // 2, NSNAP)


def draw_node_y(key, part):
    codes, lower_side = node_codes()

    def draw_one(code):
        sub_key = jax.random.fold_in(jax.random.fold_in(key, 23), code)
        return jax.random.normal(sub_key, (NSNAP, NSNAP), jnp.float32) * (NSNAP / 4.0) ** (-0.5)
    drawn = jax.vmap(draw_one)(codes)
    return drawn.reshape(GROUPS, SLOTS, LEVELS, NSNAP, NSNAP).astype(jnp.bfloat16)


def draw_leaf_map(key, part):
    flipped = jax.random.randint(key, (GROUPS, SLOTS // 2), 0, 2)
    widened = jnp.repeat(flipped, 2, axis=1)
    position = jnp.arange(SLOTS, dtype=jnp.int32)[None, :]
    return (position + widened * (1 - 2 * (position % 2))).astype(jnp.int32)


def steps_of(key, extent, cuts, low, top_value):
    factor_of, own = 1.0, jax.random.fold_in(key, 6)
    for dim, shards_of in cuts:
        steps = jnp.exp(jax.random.uniform(jax.random.fold_in(own, dim), (shards_of,), jnp.float32, low / len(cuts), top_value / len(cuts)))
        factor_of = factor_of * jnp.repeat(steps, extent[dim] // shards_of).reshape([-1 if axis == dim else 1 for axis in range(len(extent))])
    return factor_of


def normal_values(stream_key, extent, spread, limit, cuts=(), held_as=jnp.bfloat16):
    entries = jax.random.normal(stream_key, extent, jnp.float32) * spread
    if len(cuts) > 0:
        entries = steps_of(stream_key, extent, cuts, -0.22, 0.18) * entries
    return jnp.clip(entries, min=-limit, max=limit).astype(held_as)


def setup_inputs(seed: int = 0) -> dict:
    arg_keys = jax.random.split(jax.random.key(seed), 9)
    left_vectors = normal_values(arg_keys[0], (NSNAP, KVEC), 1.0, 6.0, (), jnp.float32)
    panel_vectors = normal_values(arg_keys[1], (PANELS, NSNAP, PANEL), NSNAP ** -0.5, 0.375)
    panel_factors = normal_values(arg_keys[2], (PANELS, PANEL, PANEL), PANEL ** -0.5, 0.5, (), jnp.float32)
    node_y = draw_node_y(jax.random.fold_in(arg_keys[8], 71), 0)
    node_t = draw_node_t(jax.random.fold_in(arg_keys[8], 71), 0)
    leaf_v = normal_values(arg_keys[5], (ROWS, NSNAP), NSNAP ** -0.5, 0.375, ((0, 32),))
    leaf_t = normal_values(arg_keys[6], (GROUPS, SLOTS, NSNAP, NSNAP), (4 * NSNAP) ** -0.5, 0.1875, ((0, 4), (1, 8)), jnp.float32)
    leaf_map = draw_leaf_map(jax.random.fold_in(arg_keys[8], 71), 0)
    return {"left_vectors": left_vectors, "panel_vectors": panel_vectors, "panel_factors": panel_factors, "node_y": node_y, "node_t": node_t, "leaf_v": leaf_v, "leaf_t": leaf_t, "leaf_map": leaf_map}


highest = lax.Precision.HIGHEST


def back_panels(vectors, panel_vectors, panel_factors):
    result = vectors
    panel_count = panel_vectors.shape[0]
    for panel_index in range(panel_count - 1, -1, -1):
        reflect = panel_vectors[panel_index].astype(jnp.float32)
        projected = jnp.dot(reflect.T, result, precision=highest)
        scaled = jnp.dot(panel_factors[panel_index], projected, precision=highest)
        result = result - jnp.dot(reflect, scaled, precision=highest)
    return result


def leaf_apply(operands):
    leaf_block, factor, incoming, rounded = operands
    projected = jnp.dot(leaf_block[:NSNAP].T, rounded, preferred_element_type=jnp.float32)
    solved = jnp.dot(factor, projected, precision=highest).astype(jnp.bfloat16)
    applied = jnp.dot(leaf_block, solved, preferred_element_type=jnp.float32)
    extended = jnp.concatenate([incoming, jnp.zeros((ROWS_DEV - NSNAP, KVEC), jnp.float32)], axis=0)
    return (extended - applied).astype(jnp.bfloat16)


def reference(left_vectors, panel_vectors, panel_factors, node_y, node_t, leaf_v, leaf_t, leaf_map):
    device_total = GROUPS * SLOTS
    root_vectors = back_panels(left_vectors, panel_vectors, panel_factors)
    factor_rows = node_t.reshape(device_total, LEVELS, NSNAP // 2, NSNAP)
    reflect_all = node_y.reshape(device_total, LEVELS, NSNAP, NSNAP)
    current = root_vectors[None]
    for tree_level in range(LEVELS):
        block_size = device_total // (2 ** tree_level)
        top_owners = jnp.arange(0, device_total, block_size, dtype=jnp.int32)
        bottom_owners = top_owners + block_size // 2
        factor_t = jnp.concatenate([factor_rows[top_owners, tree_level], factor_rows[bottom_owners, tree_level]], axis=1)
        factor_y = reflect_all[bottom_owners, tree_level].astype(jnp.float32)
        weighted = jnp.einsum('nij,njk->nik', factor_t, current, precision=highest)
        upper_half = current - weighted
        lower_half = -jnp.einsum('nij,njk->nik', factor_y, weighted, precision=highest)
        current = jnp.stack([upper_half, lower_half], axis=1).reshape(-1, NSNAP, KVEC)
    slot_vectors = current.reshape(GROUPS, SLOTS, NSNAP, KVEC)
    slot_numbers = jnp.broadcast_to(jnp.arange(SLOTS, dtype=jnp.int32)[None, :], (GROUPS, SLOTS))
    group_numbers = jnp.arange(GROUPS, dtype=jnp.int32)[:, None]
    inverse = jnp.zeros((GROUPS, SLOTS), jnp.int32).at[group_numbers, leaf_map].set(slot_numbers)
    device_x = slot_vectors[group_numbers, inverse].reshape(device_total, NSNAP, KVEC)
    rounded = device_x.astype(jnp.bfloat16)
    blocks = leaf_v.reshape(device_total, ROWS_DEV, NSNAP)
    factors = leaf_t.reshape(device_total, NSNAP, NSNAP)
    results = lax.map(leaf_apply, (blocks, factors, device_x, rounded))
    return results.reshape(ROWS, KVEC)
```

```python
import jax
import jax.numpy as jnp
from jax import lax
from jax.experimental import pallas as pl
from jax.experimental.pallas import tpu as pltpu
from jax.sharding import PartitionSpec as P

MESH = pl.DeviceIdType.MESH
F32, BF16 = jnp.float32, jnp.bfloat16


def halves(x):
    high = x.astype(BF16)
    return high, (x - high.astype(F32)).astype(BF16)


def dot(a, b, contract=((1,), (0,))):
    return lax.dot_general(a, b, (contract, ((), ())), preferred_element_type=F32)


def dot_exact_left(a, b, contract=((1,), (0,))):
    n = b.shape[1]
    both = dot(a, jnp.concatenate(halves(b), axis=1), contract)
    return both[:, :n] + both[:, n:]


def dot_split(a_halves, b):
    a_high, a_low = a_halves
    b_high, b_low = halves(b)
    n = b.shape[1]
    both = dot(a_high, jnp.concatenate([b_high, b_low], axis=1))
    return both[:, :n] + both[:, n:] + dot(a_low, b_high)


def kernel(group_count, slot_count, left_ref, panel_v_ref, panel_f_ref, node_y_ref, node_t_ref,
           leaf_v_ref, leaf_t_ref, map_ref, out_ref,
           left, panel_v, panel_f, node_y, factor, leaf_v, leaf_t,
           in_sem, own_sem, send_sem, recv_sem):
    group_levels = group_count.bit_length() - 1
    leaf_levels = slot_count.bit_length() - 1
    levels = group_levels + leaf_levels
    half = node_t_ref.shape[3]
    n = node_t_ref.shape[4]
    g = lax.axis_index("group")
    j = lax.axis_index("leaf")

    sides, partners = [], []
    for level in range(levels):
        if level < group_levels:
            bit = 1 << (group_levels - 1 - level)
            side = lax.rem(g // bit, 2)
            partners.append((g + bit * (1 - 2 * side), j))
        else:
            bit = 1 << (levels - 1 - level)
            side = lax.rem(j // bit, 2)
            partners.append((g, j + bit * (1 - 2 * side)))
        sides.append(side)

    barrier = pltpu.get_barrier_semaphore()
    for partner in partners:
        pl.semaphore_signal(barrier, inc=1, device_id=partner, device_id_type=MESH)

    loads = [
        pltpu.make_async_copy(source, target, in_sem.at[k])
        for k, (source, target) in enumerate([
            (left_ref, left), (panel_v_ref, panel_v), (panel_f_ref, panel_f),
            (node_y_ref.at[0, 0], node_y), (leaf_v_ref, leaf_v), (leaf_t_ref.at[0, 0], leaf_t),
        ])
    ]
    for load in loads[:3]:
        load.start()
    rows = [pl.ds(pl.multiple_of(sides[level] * half, half), half) for level in range(levels)]
    own = [
        pltpu.make_async_copy(node_t_ref.at[0, 0, level], factor.at[level, rows[level]], own_sem.at[level])
        for level in range(levels)
    ]
    sends = [
        pltpu.make_async_remote_copy(
            src_ref=node_t_ref.at[0, 0, level], dst_ref=factor.at[level, rows[level]],
            send_sem=send_sem.at[level], recv_sem=recv_sem.at[level],
            device_id=partners[level], device_id_type=MESH)
        for level in range(levels)
    ]
    pl.semaphore_wait(barrier, levels)
    first = group_levels
    order = [first, 0] + list(range(levels - 1, first, -1)) + list(range(1, group_levels))
    for level in order:
        sends[level].start()
    for load in loads[3:]:
        load.start()
    for level in range(levels):
        own[level].start()

    for load in loads[:3]:
        load.wait()
    current = left[...]
    for p in range(panel_v_ref.shape[0] - 1, -1, -1):
        reflect = panel_v[p]
        projected = dot_exact_left(reflect, current, ((0,), (0,)))
        scaled = dot_split(halves(panel_f[p]), projected)
        current = current - dot_exact_left(reflect, scaled)

    for load in loads[3:]:
        load.wait()
    for level in range(levels):
        own[level].wait()

    diagonal = (lax.broadcasted_iota(jnp.int32, (n, n), 0)
                == lax.broadcasted_iota(jnp.int32, (n, n), 1))
    identity = jnp.where(diagonal, 1.0, 0.0)
    flipped = jnp.minimum(jnp.abs(map_ref[0, 0] - j), 1)
    odd = lax.rem(j, 2)
    last = odd + flipped - 2 * odd * flipped

    lower = [side.astype(F32) for side in sides[:-1]] + [last.astype(F32)]

    def spread(level):
        f = lower[level]
        return (node_y[level].astype(F32) * f + identity * (1.0 - f)).astype(BF16)

    def step(level, x):
        weighted = dot_split(halves(factor[level]), x)
        return x * (1.0 - lower[level]) - dot_exact_left(spread(level), weighted)

    for level in range(levels):
        sends[level].wait()
        current = step(level, current)

    rounded = current.astype(BF16)
    projected = dot(leaf_v[:n], rounded, ((0,), (0,)))
    solved = dot_split(halves(leaf_t[...]), projected).astype(BF16)
    out_ref[:n] = (current - dot(leaf_v[:n], solved)).astype(BF16)
    out_ref[n:] = (-dot(leaf_v[n:], solved)).astype(BF16)


def solution(mesh):
    group_count, slot_count = mesh.shape["group"], mesh.shape["leaf"]

    def on_device(left, panel_v, panel_f, node_y, node_t, leaf_v, leaf_t, leaf_map):
        levels, n = node_y.shape[2], node_y.shape[3]
        anywhere = pl.BlockSpec(memory_space=pltpu.HBM)

        def body(*refs):
            kernel(group_count, slot_count, *refs)

        return pl.pallas_call(
            body,
            out_shape=jax.ShapeDtypeStruct((leaf_v.shape[0], left.shape[1]), BF16),
            in_specs=[anywhere] * 7 + [pl.BlockSpec(memory_space=pltpu.SMEM)],
            out_specs=pl.BlockSpec(memory_space=pltpu.VMEM),
            scratch_shapes=[
                pltpu.VMEM(left.shape, F32),
                pltpu.VMEM(panel_v.shape, BF16),
                pltpu.VMEM(panel_f.shape, F32),
                pltpu.VMEM((levels, n, n), BF16),
                pltpu.VMEM((levels, n, n), F32),
                pltpu.VMEM(leaf_v.shape, BF16),
                pltpu.VMEM((n, n), F32),
                pltpu.SemaphoreType.DMA((6,)),
                pltpu.SemaphoreType.DMA((levels,)),
                pltpu.SemaphoreType.DMA((levels,)),
                pltpu.SemaphoreType.DMA((levels,)),
            ],
            compiler_params=pltpu.CompilerParams(
                collective_id=0, has_side_effects=True, vmem_limit_bytes=64512 * 1024),
        )(left, panel_v, panel_f, node_y, node_t, leaf_v, leaf_t, leaf_map)

    return jax.shard_map(
        on_device,
        mesh=mesh,
        in_specs=(
            P(), P(), P(),
            P("group", "leaf", None, None, None),
            P("group", "leaf", None, None, None),
            P(("group", "leaf"), None),
            P("group", "leaf", None, None),
            P("group", "leaf"),
        ),
        out_specs=P(("group", "leaf"), None),
        check_vma=False,
    )
```

```python
import jax
import jax.numpy as jnp
from jax import lax
from jax.experimental import pallas as pl
from jax.experimental.pallas import tpu as pltpu
from jax.sharding import PartitionSpec as P

MESH = pl.DeviceIdType.MESH
F32, BF16 = jnp.float32, jnp.bfloat16


def halves(x):
    high = x.astype(BF16)
    return high, (x - high.astype(F32)).astype(BF16)


def dot(a, b, contract=((1,), (0,))):
    return lax.dot_general(a, b, (contract, ((), ())), preferred_element_type=F32)


def dot_exact_left(a, b, contract=((1,), (0,))):
    n = b.shape[1]
    both = dot(a, jnp.concatenate(halves(b), axis=1), contract)
    return both[:, :n] + both[:, n:]


def dot_split(a_halves, b):
    a_high, a_low = a_halves
    b_high, b_low = halves(b)
    n = b.shape[1]
    both = dot(a_high, jnp.concatenate([b_high, b_low], axis=1))
    return both[:, :n] + both[:, n:] + dot(a_low, b_high)


def kernel(group_count, slot_count, left_ref, panel_v_ref, panel_f_ref, node_y_ref, node_t_ref,
           leaf_v_ref, leaf_t_ref, map_ref, out_ref,
           left, panel_v, panel_f, node_y, factor, leaf_v, leaf_t,
           in_sem, own_sem, send_sem, recv_sem):
    group_levels = group_count.bit_length() - 1
    leaf_levels = slot_count.bit_length() - 1
    levels = group_levels + leaf_levels
    half = node_t_ref.shape[3]
    n = node_t_ref.shape[4]
    g = lax.axis_index("group")
    j = lax.axis_index("leaf")

    sides, partners = [], []
    for level in range(levels):
        if level < group_levels:
            bit = 1 << (group_levels - 1 - level)
            side = lax.rem(g // bit, 2)
            partners.append((g + bit * (1 - 2 * side), j))
        else:
            bit = 1 << (levels - 1 - level)
            side = lax.rem(j // bit, 2)
            partners.append((g, j + bit * (1 - 2 * side)))
        sides.append(side)

    barrier = pltpu.get_barrier_semaphore()
    for partner in partners:
        pl.semaphore_signal(barrier, inc=1, device_id=partner, device_id_type=MESH)

    loads = [
        pltpu.make_async_copy(source, target, in_sem.at[k])
        for k, (source, target) in enumerate([
            (left_ref, left), (panel_v_ref, panel_v), (panel_f_ref, panel_f),
            (node_y_ref.at[0, 0], node_y), (leaf_v_ref, leaf_v), (leaf_t_ref.at[0, 0], leaf_t),
        ])
    ]
    for load in loads[:3]:
        load.start()
    rows = [pl.ds(pl.multiple_of(sides[level] * half, half), half) for level in range(levels)]
    own = [
        pltpu.make_async_copy(node_t_ref.at[0, 0, level], factor.at[level, rows[level]], own_sem.at[level])
        for level in range(levels)
    ]
    first = group_levels
    quarter = half // 2
    mine = lax.rem(j, 2) * quarter

    def send(source, target, partner, slot):
        return pltpu.make_async_remote_copy(
            src_ref=source, dst_ref=target, send_sem=send_sem.at[slot], recv_sem=recv_sem.at[slot],
            device_id=partner, device_id_type=MESH)

    sends = [
        send(node_t_ref.at[0, 0, level], factor.at[level, rows[level]], partners[level], level)
        for level in range(levels)
    ]
    cross_rows = pl.ds(pl.multiple_of(sides[first] * half + mine, quarter), quarter)
    sends[first] = send(
        node_t_ref.at[0, 0, first, pl.ds(pl.multiple_of(mine, quarter), quarter)],
        factor.at[first, cross_rows], partners[first], first)
    pass_rows = factor.at[first, pl.ds(pl.multiple_of((1 - sides[first]) * half + mine, quarter), quarter)]
    passed = send(pass_rows, pass_rows, partners[levels - 1], levels)
    pl.semaphore_wait(barrier, levels)
    early = [first, 0, levels - 1] + list(range(1, group_levels))
    for level in early:
        sends[level].start()
    for level in range(first + 1, levels - 1):
        sends[level].start()
    for load in loads[3:]:
        load.start()
    for level in range(levels):
        own[level].start()

    for load in loads[:3]:
        load.wait()
    current = left[...]
    for p in range(panel_v_ref.shape[0] - 1, -1, -1):
        reflect = panel_v[p]
        projected = dot_exact_left(reflect, current, ((0,), (0,)))
        scaled = dot_split(halves(panel_f[p]), projected)
        current = current - dot_exact_left(reflect, scaled)

    for load in loads[3:]:
        load.wait()
    for level in range(levels):
        own[level].wait()

    diagonal = (lax.broadcasted_iota(jnp.int32, (n, n), 0)
                == lax.broadcasted_iota(jnp.int32, (n, n), 1))
    identity = jnp.where(diagonal, 1.0, 0.0)
    flipped = jnp.minimum(jnp.abs(map_ref[0, 0] - j), 1)
    odd = lax.rem(j, 2)
    last = odd + flipped - 2 * odd * flipped

    lower = [side.astype(F32) for side in sides[:-1]] + [last.astype(F32)]

    def spread(level):
        f = lower[level]
        return (node_y[level].astype(F32) * f + identity * (1.0 - f)).astype(BF16)

    def step(level, x):
        weighted = dot_split(halves(factor[level]), x)
        return x * (1.0 - lower[level]) - dot_exact_left(spread(level), weighted)

    def whole_step(level):
        return identity * (1.0 - lower[level]) - dot_exact_left(spread(level), factor[level])

    top = leaf_v[:n]
    solver_high, solver_low = halves(leaf_t[...])
    solver = dot(solver_high, top, ((1,), (1,))) + dot(solver_low, top, ((1,), (1,)))
    solver_high, solver_low = halves(solver)

    sends[first].wait_recv()
    passed.start()
    for level in range(first):
        sends[level].wait()
        current = step(level, current)
    rest = None
    for level in range(levels - 1, first, -1):
        sends[level].wait()
        one = whole_step(level)
        rest = halves(one if rest is None else dot_split(rest, one))
    sends[first].wait_send()
    passed.wait()
    current = dot_split(rest, step(first, current))

    rounded = current.astype(BF16)
    solved = (dot(solver_high, rounded) + dot(solver_low, rounded)).astype(BF16)
    out_ref[:n] = (current - dot(leaf_v[:n], solved)).astype(BF16)
    out_ref[n:] = (-dot(leaf_v[n:], solved)).astype(BF16)


def solution(mesh):
    group_count, slot_count = mesh.shape["group"], mesh.shape["leaf"]

    def on_device(left, panel_v, panel_f, node_y, node_t, leaf_v, leaf_t, leaf_map):
        levels, n = node_y.shape[2], node_y.shape[3]
        anywhere = pl.BlockSpec(memory_space=pltpu.HBM)

        pin = lambda x: pltpu.with_memory_space_constraint(x, pltpu.HBM)

        def body(*refs):
            kernel(group_count, slot_count, *refs)

        return pl.pallas_call(
            body,
            out_shape=jax.ShapeDtypeStruct((leaf_v.shape[0], left.shape[1]), BF16),
            in_specs=[anywhere] * 7 + [pl.BlockSpec(memory_space=pltpu.SMEM)],
            out_specs=pl.BlockSpec(memory_space=pltpu.VMEM),
            scratch_shapes=[
                pltpu.VMEM(left.shape, F32),
                pltpu.VMEM(panel_v.shape, BF16),
                pltpu.VMEM(panel_f.shape, F32),
                pltpu.VMEM((levels, n, n), BF16),
                pltpu.VMEM((levels, n, n), F32),
                pltpu.VMEM(leaf_v.shape, BF16),
                pltpu.VMEM((n, n), F32),
                pltpu.SemaphoreType.DMA((6,)),
                pltpu.SemaphoreType.DMA((levels,)),
                pltpu.SemaphoreType.DMA((levels + 1,)),
                pltpu.SemaphoreType.DMA((levels + 1,)),
            ],
            compiler_params=pltpu.CompilerParams(
                collective_id=0, has_side_effects=True, vmem_limit_bytes=40 * 1024 * 1024),
        )(*map(pin, (left, panel_v, panel_f, node_y, node_t, leaf_v, leaf_t)), leaf_map)

    return jax.shard_map(
        on_device,
        mesh=mesh,
        in_specs=(
            P(), P(), P(),
            P("group", "leaf", None, None, None),
            P("group", "leaf", None, None, None),
            P(("group", "leaf"), None),
            P("group", "leaf", None, None),
            P("group", "leaf"),
        ),
        out_specs=P(("group", "leaf"), None),
        check_vma=False,
    )
```

```python
import jax
import jax.numpy as jnp
from jax import lax
from jax.experimental import pallas as pl
from jax.experimental.pallas import tpu as pltpu
from jax.sharding import PartitionSpec as P

MESH = pl.DeviceIdType.MESH
F32, BF16 = jnp.float32, jnp.bfloat16
PIECES = 4


def halves(x):
    high = x.astype(BF16)
    return high, (x - high.astype(F32)).astype(BF16)


def dot(a, b, contract=((1,), (0,))):
    return lax.dot_general(a, b, (contract, ((), ())), preferred_element_type=F32)


def dot_exact_left(a, b, contract=((1,), (0,))):
    n = b.shape[1]
    both = dot(a, jnp.concatenate(halves(b), axis=1), contract)
    return both[:, :n] + both[:, n:]


def dot_split(a_halves, b):
    a_high, a_low = a_halves
    b_high, b_low = halves(b)
    n = b.shape[1]
    both = dot(a_high, jnp.concatenate([b_high, b_low], axis=1))
    return both[:, :n] + both[:, n:] + dot(a_low, b_high)


def kernel(group_count, slot_count, left_ref, panel_v_ref, panel_f_ref, node_y_ref, node_t_ref,
           leaf_v_ref, leaf_t_ref, map_ref, out_ref,
           left, panel_v, panel_f, node_y, factor, leaf_v, leaf_t,
           in_sem, own_sem, send_sem, recv_sem):
    group_levels = group_count.bit_length() - 1
    leaf_levels = slot_count.bit_length() - 1
    levels = group_levels + leaf_levels
    half = node_t_ref.shape[3]
    n = node_t_ref.shape[4]
    g = lax.axis_index("group")
    j = lax.axis_index("leaf")

    sides, partners = [], []
    for level in range(levels):
        if level < group_levels:
            bit = 1 << (group_levels - 1 - level)
            side = lax.rem(g // bit, 2)
            partners.append((g + bit * (1 - 2 * side), j))
        else:
            bit = 1 << (levels - 1 - level)
            side = lax.rem(j // bit, 2)
            partners.append((g, j + bit * (1 - 2 * side)))
        sides.append(side)

    barrier = pltpu.get_barrier_semaphore()
    for partner in partners:
        pl.semaphore_signal(barrier, inc=1, device_id=partner, device_id_type=MESH)

    loads = [
        pltpu.make_async_copy(source, target, in_sem.at[k])
        for k, (source, target) in enumerate([
            (left_ref, left), (panel_v_ref, panel_v), (panel_f_ref, panel_f),
            (node_y_ref.at[0, 0], node_y), (leaf_v_ref, leaf_v), (leaf_t_ref.at[0, 0], leaf_t),
        ])
    ]
    rows = [pl.ds(pl.multiple_of(sides[level] * half, half), half) for level in range(levels)]
    own = [
        pltpu.make_async_copy(node_t_ref.at[0, 0, level], factor.at[level, rows[level]], own_sem.at[level])
        for level in range(levels)
    ]
    for level in [group_levels, 0, levels - 1] + list(range(1, group_levels)) + list(range(group_levels + 1, levels - 1)):
        own[level].start()
    for load in loads[:3]:
        load.start()

    first = group_levels
    quarter = half // 2

    def send(source, target, partner, slot):
        return pltpu.make_async_remote_copy(
            src_ref=source, dst_ref=target, send_sem=send_sem.at[slot], recv_sem=recv_sem.at[slot],
            device_id=partner, device_id_type=MESH)

    def relay(level, pair_level, pieces, slot):
        piece = quarter // pieces
        crossed, passed = [], []
        for k in range(pieces):
            begin = sides[pair_level] * quarter + k * piece
            leaving = factor.at[level, pl.ds(pl.multiple_of(sides[level] * half + begin, piece), piece)]
            arrived = factor.at[level, pl.ds(pl.multiple_of((1 - sides[level]) * half + begin, piece), piece)]
            crossed.append(send(leaving, leaving, partners[level], slot + k))
            passed.append(send(arrived, arrived, partners[pair_level], slot + pieces + k))
        return crossed, passed

    sends = [
        send(factor.at[level, rows[level]], factor.at[level, rows[level]], partners[level], level)
        if level != first else None
        for level in range(levels)
    ]
    crossed, passed = relay(first, levels - 1, PIECES, levels)
    pl.semaphore_wait(barrier, levels)
    own[first].wait()
    for copy in crossed:
        copy.start()
    early = [0, levels - 1] + list(range(1, group_levels))
    for level in early:
        own[level].wait()
        sends[level].start()
    for level in range(first + 1, levels - 1):
        own[level].wait()
        sends[level].start()
    for load in loads[3:]:
        load.start()

    for load in loads[:3]:
        load.wait()
    current = left[...]
    for p in range(panel_v_ref.shape[0] - 1, -1, -1):
        reflect = panel_v[p]
        projected = dot_exact_left(reflect, current, ((0,), (0,)))
        scaled = dot_split(halves(panel_f[p]), projected)
        current = current - dot_exact_left(reflect, scaled)

    for load in loads[3:]:
        load.wait()

    diagonal = (lax.broadcasted_iota(jnp.int32, (n, n), 0)
                == lax.broadcasted_iota(jnp.int32, (n, n), 1))
    identity = jnp.where(diagonal, 1.0, 0.0)
    flipped = jnp.minimum(jnp.abs(map_ref[0, 0] - j), 1)
    odd = lax.rem(j, 2)
    last = odd + flipped - 2 * odd * flipped

    lower = [side.astype(F32) for side in sides[:-1]] + [last.astype(F32)]

    def spread(level):
        f = lower[level]
        return (node_y[level].astype(F32) * f + identity * (1.0 - f)).astype(BF16)

    def step(level, x):
        weighted = dot_split(halves(factor[level]), x)
        return x * (1.0 - lower[level]) - dot_exact_left(spread(level), weighted)

    def whole_step(level):
        return identity * (1.0 - lower[level]) - dot_exact_left(spread(level), factor[level])

    top = leaf_v[:n]
    solver_high, solver_low = halves(leaf_t[...])
    solver = dot(solver_high, top, ((1,), (1,))) + dot(solver_low, top, ((1,), (1,)))
    solver_high, solver_low = halves(solver)

    for k in range(PIECES):
        crossed[k].wait_recv()
        passed[k].start()
    for level in range(first):
        sends[level].wait()
        current = step(level, current)
    rest = None
    for level in range(levels - 1, first, -1):
        sends[level].wait()
        one = whole_step(level)
        rest = halves(one if rest is None else dot_split(rest, one))
    kept = dot_split(rest, current) * (1.0 - lower[first])
    onward = halves(dot(rest[0], spread(first)) + dot(rest[1], spread(first)))
    for copy in crossed:
        copy.wait_send()
    for copy in passed:
        copy.wait()
    current = kept - dot_split(onward, dot_split(halves(factor[first]), current))

    rounded = current.astype(BF16)
    solved = (dot(solver_high, rounded) + dot(solver_low, rounded)).astype(BF16)
    out_ref[:n] = (current - dot(leaf_v[:n], solved)).astype(BF16)
    out_ref[n:] = (-dot(leaf_v[n:], solved)).astype(BF16)


def solution(mesh):
    group_count, slot_count = mesh.shape["group"], mesh.shape["leaf"]

    def on_device(left, panel_v, panel_f, node_y, node_t, leaf_v, leaf_t, leaf_map):
        levels, n = node_y.shape[2], node_y.shape[3]
        anywhere = pl.BlockSpec(memory_space=pltpu.HBM)

        pin = lambda x: pltpu.with_memory_space_constraint(x, pltpu.HBM)

        def body(*refs):
            kernel(group_count, slot_count, *refs)

        return pl.pallas_call(
            body,
            out_shape=jax.ShapeDtypeStruct((leaf_v.shape[0], left.shape[1]), BF16),
            in_specs=[anywhere] * 7 + [pl.BlockSpec(memory_space=pltpu.SMEM)],
            out_specs=pl.BlockSpec(memory_space=pltpu.VMEM),
            scratch_shapes=[
                pltpu.VMEM(left.shape, F32),
                pltpu.VMEM(panel_v.shape, BF16),
                pltpu.VMEM(panel_f.shape, F32),
                pltpu.VMEM((levels, n, n), BF16),
                pltpu.VMEM((levels, n, n), F32),
                pltpu.VMEM(leaf_v.shape, BF16),
                pltpu.VMEM((n, n), F32),
                pltpu.SemaphoreType.DMA((6,)),
                pltpu.SemaphoreType.DMA((levels,)),
                pltpu.SemaphoreType.DMA((levels + 2 * PIECES,)),
                pltpu.SemaphoreType.DMA((levels + 2 * PIECES,)),
            ],
            compiler_params=pltpu.CompilerParams(
                collective_id=0, has_side_effects=True, vmem_limit_bytes=40 * 1024 * 1024),
        )(*map(pin, (left, panel_v, panel_f, node_y, node_t, leaf_v, leaf_t)), leaf_map)

    return jax.shard_map(
        on_device,
        mesh=mesh,
        in_specs=(
            P(), P(), P(),
            P("group", "leaf", None, None, None),
            P("group", "leaf", None, None, None),
            P(("group", "leaf"), None),
            P("group", "leaf", None, None),
            P("group", "leaf"),
        ),
        out_specs=P(("group", "leaf"), None),
        check_vma=False,
    )
```
